256 devices in a mesh: frame: 32 (over z, y_hi, core), fsdp: 8 (over y_lo, x).
Axes of the slice: x: 4, y: 4 (y_hi: 2, y_lo: 2; y = y_hi * 2 + y_lo), z: 8, core: 2. Of those that a mesh axis runs over, the one named last changes fastest.
Arguments:
- query_rows: bfloat16 [8, 4096, 1536], P('fsdp', 'frame'), may hold values from -96 to 96
- key_rows: bfloat16 [8, 4096, 1536], P('fsdp', 'frame'), may hold values from -4 to 4
- value_rows: bfloat16 [8, 4096, 1536], P('fsdp', 'frame'), may hold values from -6 to 6
- frame_of: int32 [8, 32], P('fsdp', 'frame'), may hold values from 0 to 15, never falling along the last dimension, each value on 1 to 4 neighbouring positions
- reach_back: int32 [8, 32], P('fsdp', 'frame'), may hold values from 0 to 2
- reach_ahead: int32 [8, 32], P('fsdp', 'frame'), may hold values from 0 to 2
- out_weight: bfloat16 [1536, 1536], P('fsdp'), may hold values from -0.15625 to 0.15625
- out_grad: bfloat16 [8, 4096, 1536], P('fsdp', 'frame'), may hold values from -6 to 6
Outputs:
- layer_out: bfloat16 [8, 4096, 1536], P('fsdp', 'frame')
- grad_query: bfloat16 [8, 4096, 1536], P('fsdp', 'frame')
- grad_key: bfloat16 [8, 4096, 1536], P('fsdp', 'frame')
- grad_value: bfloat16 [8, 4096, 1536], P('fsdp', 'frame')
- grad_weight: float32 [1536, 1536], P(('frame', 'fsdp'))
The draws below stay inside these ranges and needn't reach their ends.
Inputs may be any that keep to these rules, and one draw needn't show every extreme that they name: `frame_of`: frame numbers never fall along a clip's tiles; each frame covers 1 to 4 tiles.
All inputs are finite; a program needn't handle non-finite values.
Results may differ from the reference program's by a relative error of at most 0.03.
Values may be sent and summed in bfloat16 or wider, within the bound.
No kernel may reach another device: no remote copies, remote signals or barrier semaphores. Data moves between devices by JAX's collectives and lax.ppermute only.
A program may use at most 128 MiB of HBM per device.

```python
import math
import jax
import jax.numpy as jnp
import numpy as np
from jax import lax

HEADS = 12
HEAD_DIM = 128
D_OUT = 1536
TILE = 128
HD = 1536
SPAN = 1
TOKENS = 4096
TILES_ALL = 32
FRAMES = 16
CLIPS = 8


def shared_rows(key):
    return jnp.clip(jax.random.normal(key, (CLIPS, TOKENS, HD), jnp.float32), -4.0, 4.0)


def draw_key_rows(key, part):
    base = shared_rows(key)
    return base.astype(jnp.bfloat16)


def draw_query_rows(key, part):
    base = shared_rows(key)
    key = jax.random.fold_in(key, 5)
    own_rows = jnp.clip(0.5 * jax.random.normal(key, base.shape, jnp.float32), -3.0, 3.0)
    return own_rows.astype(jnp.bfloat16)


def set_ends(values, rng, least, high):
    longest = values.shape.index(max(values.shape))
    spots = []
    for shift in (0, 1):
        where = [jax.random.randint(jax.random.fold_in(rng, axis), (), 0, length) for axis, length in enumerate(values.shape)]
        where[longest] = (where[longest] + shift) % values.shape[longest]
        spots.append(tuple(where))
    return values.at[spots[0]].set(least).at[spots[1]].set(high)


def level_of(rng, dims, cuts, low, largest):
    gain, own = 1.0, jax.random.fold_in(rng, 6)
    for axis_at, shards_of in cuts:
        heights = jnp.exp(jax.random.uniform(jax.random.fold_in(own, axis_at), (shards_of,), jnp.float32, low / len(cuts), largest / len(cuts)))
        gain = gain * jnp.repeat(heights, dims[axis_at] // shards_of).reshape([-1 if axis == axis_at else 1 for axis in range(len(dims))])
    return gain


def split_up(amount, total, bound, slope):
    portions = [(1 << 20) // math.isqrt(rank ** slope) + 1 for rank in range(2, amount + 1)]
    rest, counts = total - bound - (amount - 1), [1] * (amount - 1)
    while rest > 0:
        free = [i for i in range(amount - 1) if counts[i] < bound]
        mass, left = sum([portions[i] for i in free]), rest
        for i in free:
            extra = min(bound - counts[i], max(1, left * portions[i] // mass), rest)
            counts[i] = counts[i] + extra
            rest = rest - extra
    return np.array([bound] + counts)


def ragged(own_key, amount, total, limit, lean):
    if amount == 2:
        one = jax.random.randint(own_key, (), max(1, total - limit), min(limit, total - 1) + 1)
        return jnp.stack([one, total - one])
    sizes = jnp.asarray(split_up(amount, total, limit, lean), jnp.int32)
    couples = (amount - 1) // 2
    donor, sink = sizes[1:1 + 2 * couples:2], sizes[2:2 + 2 * couples:2]
    slack = jnp.minimum(donor - 1, limit - sink)
    passed = jax.random.randint(jax.random.fold_in(own_key, 1), (couples,), 0, 1 << 20) % (slack + 1)
    sizes = sizes.at[1:1 + 2 * couples:2].set(donor - passed).at[2:2 + 2 * couples:2].set(sink + passed)
    return sizes[jax.random.permutation(jax.random.fold_in(own_key, 2), amount)]


def gaussian(key, shape, spread, bound, shards=(), held_as=jnp.bfloat16):
    values = spread * jax.random.normal(key, shape, jnp.float32)
    if shards:
        values = values * level_of(key, shape, shards, -0.22, 0.18)
    return jnp.clip(values, -bound, bound).astype(held_as)


def setup_inputs(seed: int = 0) -> dict:
    arg_keys = jax.random.split(jax.random.key(seed), 9)
    query_rows = draw_query_rows(jax.random.fold_in(arg_keys[8], 71), 0)
    key_rows = draw_key_rows(jax.random.fold_in(arg_keys[8], 71), 0)
    value_rows = gaussian(arg_keys[2], (CLIPS, TOKENS, HD), 1.0, 6.0, ((0, 8), (1, 32)))
    frame_of = jax.vmap(lambda own: jnp.searchsorted(jnp.cumsum(ragged(own, FRAMES, TILES_ALL, 4, 0)), jnp.arange(TILES_ALL), side="right"))(jax.random.split(arg_keys[3], CLIPS)).reshape((CLIPS, TILES_ALL)).astype(jnp.int32)
    reach_back = set_ends(jax.random.randint(arg_keys[4], (CLIPS, TILES_ALL), 0, 3), jax.random.fold_in(arg_keys[4], 1), 0, 2).astype(jnp.int32)
    reach_ahead = set_ends(jax.random.randint(arg_keys[5], (CLIPS, TILES_ALL), 0, 3), jax.random.fold_in(arg_keys[5], 1), 0, 2).astype(jnp.int32)
    out_weight = gaussian(arg_keys[6], (HD, D_OUT), HD ** -0.5, 0.15625, ((0, 8),))
    out_grad = gaussian(arg_keys[7], (CLIPS, TOKENS, D_OUT), 1.0, 6.0, ((0, 8), (1, 32)))
    return dict(query_rows=query_rows, key_rows=key_rows, value_rows=value_rows, frame_of=frame_of, reach_back=reach_back, reach_ahead=reach_ahead, out_weight=out_weight, out_grad=out_grad)


masked_score = -1.0e30


def widened(array):
    return lax.optimization_barrier(array).astype(jnp.float32)


def window(array, center):
    return lax.dynamic_slice_in_dim(array, center, 2 * SPAN + 1, 0)


def pad_tiles(array):
    return jnp.pad(array, [(SPAN, SPAN)] + [(0, 0)] * (array.ndim - 1))


def in_reach(query_frame, back_frames, ahead_frames, key_frame):
    return (key_frame >= query_frame - back_frames) & (key_frame <= query_frame + ahead_frames)


def reference(query_rows, key_rows, value_rows, frame_of, reach_back, reach_ahead, out_weight, out_grad):
    score_scale = HEAD_DIM ** -0.5
    tile_shape = (TILES_ALL, TILE, HEADS, HEAD_DIM)

    def one_clip(inputs):
        queries, keys_in, values_in, frames, backs, aheads, grad_out = inputs
        query_tiles = queries.reshape(tile_shape)
        key_tiles = keys_in.reshape(tile_shape)
        value_tiles = values_in.reshape(tile_shape)
        query_padded = pad_tiles(query_tiles)
        key_padded = pad_tiles(key_tiles)
        value_padded = pad_tiles(value_tiles)
        frames_padded = pad_tiles(frames)
        backs_padded = pad_tiles(backs)
        aheads_padded = pad_tiles(aheads)
        valid_padded = pad_tiles(jnp.ones((TILES_ALL,), jnp.int32))
        tile_ids = jnp.arange(TILES_ALL, dtype=jnp.int32)

        def tile_scores(tile_index):
            key_block = window(key_padded, tile_index).reshape(-1, HEADS, HEAD_DIM)
            value_block = window(value_padded, tile_index).reshape(-1, HEADS, HEAD_DIM)
            reach_ok = (window(valid_padded, tile_index) > 0) & in_reach(
                frames[tile_index], backs[tile_index], aheads[tile_index], window(frames_padded, tile_index))
            key_mask = jnp.repeat(reach_ok, TILE)
            scores = jnp.einsum('qhd,khd->hqk', query_tiles[tile_index].astype(jnp.float32),
                                key_block.astype(jnp.float32)) * score_scale
            scores = jnp.where(key_mask[None, None, :], scores, masked_score)
            return key_block, value_block, scores

        def forward_tile(tile_index):
            key_block, value_block, scores = tile_scores(tile_index)
            row_max = jnp.max(scores, -1)
            logsum = row_max + jnp.log(jnp.sum(jnp.exp(scores - row_max[..., None]), -1))
            probs_low = jnp.exp(scores - logsum[..., None]).astype(jnp.bfloat16)
            attended = jnp.einsum('hqk,khd->qhd', widened(probs_low), value_block.astype(jnp.float32))
            return attended.astype(jnp.bfloat16), logsum

        attended_tiles, logsum_tiles = lax.map(forward_tile, tile_ids)
        attended = attended_tiles.reshape(TOKENS, HD)
        layer_out = jnp.dot(attended, out_weight, preferred_element_type=jnp.float32).astype(jnp.bfloat16)
        grad_attended = jnp.dot(grad_out, out_weight.T, preferred_element_type=jnp.float32).astype(jnp.bfloat16)
        delta_tiles = jnp.sum((widened(grad_attended) * widened(attended)).reshape(tile_shape), -1)
        delta_tiles = jnp.transpose(delta_tiles, (0, 2, 1))
        grad_tiles = grad_attended.reshape(tile_shape)
        grad_padded = pad_tiles(grad_tiles)
        logsum_padded = pad_tiles(logsum_tiles)
        delta_padded = pad_tiles(delta_tiles)

        def query_grad_tile(tile_index):
            key_block, value_block, scores = tile_scores(tile_index)
            probs = jnp.exp(scores - logsum_tiles[tile_index][..., None])
            grad_probs = jnp.einsum('qhd,khd->hqk', grad_tiles[tile_index].astype(jnp.float32),
                                    value_block.astype(jnp.float32))
            grad_scores = (probs * (grad_probs - delta_tiles[tile_index][..., None]) * score_scale).astype(jnp.bfloat16)
            query_grad = jnp.einsum('hqk,khd->qhd', widened(grad_scores), key_block.astype(jnp.float32))
            return query_grad.astype(jnp.bfloat16)

        def key_grad_tile(tile_index):
            query_block = window(query_padded, tile_index).reshape(-1, HEADS, HEAD_DIM)
            grad_block = window(grad_padded, tile_index).reshape(-1, HEADS, HEAD_DIM)
            logsum_block = jnp.transpose(window(logsum_padded, tile_index), (1, 0, 2)).reshape(HEADS, -1)
            delta_block = jnp.transpose(window(delta_padded, tile_index), (1, 0, 2)).reshape(HEADS, -1)
            reach_ok = (window(valid_padded, tile_index) > 0) & in_reach(
                window(frames_padded, tile_index), window(backs_padded, tile_index),
                window(aheads_padded, tile_index), frames[tile_index])
            row_mask = jnp.repeat(reach_ok, TILE)
            scores = jnp.einsum('qhd,khd->hqk', query_block.astype(jnp.float32),
                                key_tiles[tile_index].astype(jnp.float32)) * score_scale
            scores = jnp.where(row_mask[None, :, None], scores, masked_score)
            probs = jnp.exp(scores - logsum_block[..., None])
            probs_low = probs.astype(jnp.bfloat16)
            value_grad = jnp.einsum('hqk,qhd->khd', widened(probs_low), grad_block.astype(jnp.float32))
            grad_probs = jnp.einsum('qhd,khd->hqk', grad_block.astype(jnp.float32),
                                    value_tiles[tile_index].astype(jnp.float32))
            grad_scores = (probs * (grad_probs - delta_block[..., None]) * score_scale).astype(jnp.bfloat16)
            key_grad = jnp.einsum('hqk,qhd->khd', widened(grad_scores), query_block.astype(jnp.float32))
            return key_grad.astype(jnp.bfloat16), value_grad.astype(jnp.bfloat16)

        query_grads = lax.map(query_grad_tile, tile_ids).reshape(TOKENS, HD)
        key_grads, value_grads = lax.map(key_grad_tile, tile_ids)
        weight_term = jnp.dot(attended.T, grad_out, preferred_element_type=jnp.float32)
        return (layer_out, query_grads, key_grads.reshape(TOKENS, HD), value_grads.reshape(TOKENS, HD), weight_term)

    results = lax.map(one_clip, (query_rows, key_rows, value_rows, frame_of, reach_back, reach_ahead, out_grad))
    grad_weight = jnp.sum(results[4], 0) * (float(CLIPS * TOKENS) ** -0.5)
    return (results[0], results[1], results[2], results[3], grad_weight)
```

```python
import jax
import jax.numpy as jnp
import numpy as np
from jax import lax
from jax.experimental import pallas as pl
from jax.experimental.pallas import tpu as pltpu
from jax.sharding import PartitionSpec as P

HEADS = 12
HEAD_DIM = 128
TILE = 128
HD = HEADS * HEAD_DIM
SCALE = HEAD_DIM**-0.5
MASKED = -1e30

SIZES = (8, 2, 2, 2, 4)
NAMES = ("z", "yhi", "core", "ylo", "x")
FRAME = ("z", "yhi", "core")
FSDP = ("ylo", "x")
TILES = 32
ROWS_OUT = 6
GROUP = 8
GROUP_ROWS = HD // GROUP

F32 = jnp.float32
BF16 = jnp.bfloat16
VMEM = pltpu.VMEM
NT = (((1,), (1,)), ((), ()))
NN = (((1,), (0,)), ((), ()))
TN = (((0,), (0,)), ((), ()))


def dot(a, b, dims=NN):
    return lax.dot_general(a, b, dims, preferred_element_type=F32)


def next_tile(value, step):
    return lax.ppermute(value, FRAME, [(i, (i + step) % TILES) for i in range(TILES)])


def core_swap(value):
    return lax.ppermute(value, "core", [(0, 1), (1, 0)])


def gather_x(value):
    spread = jnp.broadcast_to(value[None], (4,) + value.shape)
    return lax.all_to_all(spread, "x", 0, 0, tiled=True)


def head(h):
    return slice(h * HEAD_DIM, (h + 1) * HEAD_DIM)


def biases(meta, position):
    def sees(q, k):
        frame = meta[q, 0]
        return (meta[k, 0] >= frame - meta[q, 1]) & (meta[k, 0] <= frame + meta[q, 2])

    has = (position > 0, None, position < TILES - 1)
    out = {}
    for t in (0, 2):
        out["row", t] = jnp.where(sees(1, t) & has[t], 0.0, MASKED).astype(F32)
        out["col", t] = jnp.where(sees(t, 1) & has[t], 0.0, MASKED).astype(F32)
    return out


def forward_kernel(meta, pos, q, kl, ko, kr, vl, vo, vr, order, att, att_t, stats):
    bias = biases(meta, pos[0])
    lane = lax.broadcasted_iota(jnp.int32, (TILE, 128), 1)
    total = jnp.zeros((TILE, 128), F32)
    for h in range(HEADS):
        c = head(h)
        qh = q[:, c]
        sl = dot(qh, kl[:, c], NT) * SCALE + bias["row", 0]
        so = dot(qh, ko[:, c], NT) * SCALE
        sr = dot(qh, kr[:, c], NT) * SCALE + bias["row", 2]
        top = jnp.max(jnp.maximum(jnp.maximum(sl, so), sr), axis=1, keepdims=True)
        el, eo, er = jnp.exp(sl - top), jnp.exp(so - top), jnp.exp(sr - top)
        mass = jnp.sum(el + eo + er, axis=1, keepdims=True)
        inv = 1.0 / mass
        out = dot((el * inv).astype(BF16), vl[:, c])
        out += dot((eo * inv).astype(BF16), vo[:, c])
        out += dot((er * inv).astype(BF16), vr[:, c])
        att[:, c] = out.astype(BF16)
        total = jnp.where(lane == h, top + jnp.log(mass), total)
    stats[...] = total
    for g in range(GROUP):
        cols = slice(g * GROUP_ROWS, (g + 1) * GROUP_ROWS)
        moved = lax.dot_general(
            order[cols, :], att[...], NT, preferred_element_type=F32
        )
        att_t[g] = moved.astype(BF16)


def weight_kernel(core, att_t, og_mine, og_other, out):
    c = core[0]
    acc = jnp.zeros((GROUP_ROWS, HD), F32)
    for j in range(4):
        acc += dot(att_t[c * 4 + j], og_mine[j])
        acc += dot(att_t[(1 - c) * 4 + j], og_other[j])
    out[...] = (acc * float(GROUP * TILES * TILE) ** -0.5).astype(BF16)


def grad_attended_kernel(core, w_mine, w_other, ogl, ogo, ogr, att, stats, gal, gao, gar, out):
    c = core[0]
    lane = lax.broadcasted_iota(jnp.int32, (TILE, 128), 1)
    total = stats[...]
    half = HD // 2
    for side, w in ((c, w_mine), (1 - c, w_other)):
        for i in range(HEADS // 2):
            block = w[i * HEAD_DIM : (i + 1) * HEAD_DIM, :]
            cols = pl.ds(pl.multiple_of(side * half + i * HEAD_DIM, HEAD_DIM), HEAD_DIM)
            gal[:, cols] = dot(ogl[...], block, NT).astype(BF16)
            gar[:, cols] = dot(ogr[...], block, NT).astype(BF16)
            own = dot(ogo[...], block, NT).astype(BF16)
            gao[:, cols] = own
            delta = jnp.sum(own.astype(F32) * att[:, cols].astype(F32), axis=1, keepdims=True)
            total = jnp.where(lane == HEADS + side * (HEADS // 2) + i, delta, total)
    out[...] = total


def project_kernel(core, w_mine, w_other, att, out):
    half = HD // 2
    c = core[0]
    mine = att[:, pl.ds(pl.multiple_of(c * half, half), half)]
    other = att[:, pl.ds(pl.multiple_of((1 - c) * half, half), half)]
    out[...] = (dot(mine, w_mine[...]) + dot(other, w_other[...])).astype(BF16)


def pair_grads(qh, kh, vh, gh, lse, delta, bias):
    s = dot(qh, kh, NT) * SCALE
    if bias is not None:
        s = s + bias
    p = jnp.exp(s - lse)
    dp = dot(gh, vh, NT)
    ds = (p * (dp - delta) * SCALE).astype(BF16)
    return p.astype(BF16), ds


def row_kernel(meta, pos, q, kl, ko, kr, vl, vo, vr, ga, stats, dq, dk, dv):
    bias = biases(meta, pos[0])
    st = stats[...]
    for h in range(HEADS):
        c = head(h)
        qh, gh = q[:, c], ga[:, c]
        lse, delta = st[:, h : h + 1], st[:, HEADS + h : HEADS + h + 1]
        _, dsl = pair_grads(qh, kl[:, c], vl[:, c], gh, lse, delta, bias["row", 0])
        po, dso = pair_grads(qh, ko[:, c], vo[:, c], gh, lse, delta, None)
        _, dsr = pair_grads(qh, kr[:, c], vr[:, c], gh, lse, delta, bias["row", 2])
        dq[:, c] = (dot(dsl, kl[:, c]) + dot(dso, ko[:, c]) + dot(dsr, kr[:, c])).astype(BF16)
        dk[:, c] = dot(dso, qh, TN)
        dv[:, c] = dot(po, gh, TN)


def column_kernel(meta, pos, ql, qr, ko, vo, gal, gar, sl, sr, dk0, dv0, dk, dv):
    bias = biases(meta, pos[0])
    stl, str_ = sl[...], sr[...]
    for h in range(HEADS):
        c = head(h)
        kh, vh = ko[:, c], vo[:, c]
        dkh, dvh = dk0[:, c], dv0[:, c]
        for q, g, st, t in ((ql, gal, stl, 0), (qr, gar, str_, 2)):
            qh, gh = q[:, c], g[:, c]
            lse, delta = st[:, h : h + 1], st[:, HEADS + h : HEADS + h + 1]
            p, ds = pair_grads(qh, kh, vh, gh, lse, delta, bias["col", t])
            dkh = dkh + dot(ds, qh, TN)
            dvh = dvh + dot(p, gh, TN)
        dk[:, c] = dkh.astype(BF16)
        dv[:, c] = dvh.astype(BF16)


def call(kernel, scalars, arrays, outs, flops, cost_bytes, trans=0):
    return pl.pallas_call(
        kernel,
        in_specs=[pl.BlockSpec(memory_space=pltpu.SMEM)] * len(scalars)
        + [pl.BlockSpec(memory_space=VMEM)] * len(arrays),
        out_specs=[pl.BlockSpec(memory_space=VMEM)] * len(outs),
        out_shape=[jax.ShapeDtypeStruct(s, d) for s, d in outs],
        cost_estimate=pl.CostEstimate(flops=flops, bytes_accessed=cost_bytes, transcendentals=trans),
        compiler_params=pltpu.CompilerParams(vmem_limit_bytes=40 * 1024 * 1024),
    )(*scalars, *arrays)


def column_order():
    features = np.arange(HD).reshape(SIZES + (ROWS_OUT,))
    return features.transpose(2, 4, 0, 1, 3, 5).reshape(-1)


def shards(query_rows, key_rows, value_rows, frame_of, reach_back, reach_ahead, out_weight, out_grad):
    position = lax.axis_index(FRAME)
    core = lax.axis_index("core")
    q, k, v, og = query_rows[0], key_rows[0], value_rows[0], out_grad[0]
    tile = (TILE, HD)
    small = (TILE, 128)
    pos = position.astype(jnp.int32).reshape(1)
    which = core.astype(jnp.int32).reshape(1)

    own_meta = jnp.stack([frame_of[0, 0], reach_back[0, 0], reach_ahead[0, 0]])
    meta_l, meta_r = next_tile(own_meta, 1), next_tile(own_meta, -1)
    meta = jnp.stack([meta_l, own_meta, meta_r])
    kl, kr = next_tile(k, 1), next_tile(k, -1)
    vl, vr = next_tile(v, 1), next_tile(v, -1)

    og_mine = gather_x(og)
    og_other = core_swap(og_mine)

    half_index = core * 2 + lax.axis_index("ylo")
    passed = lax.ppermute(out_weight, ("core", "ylo"), [(0, 1), (3, 2)])
    chosen = jnp.where((half_index == 0) | (half_index == 3), out_weight, passed)
    w_mine = gather_x(chosen).reshape(HD // 2, HD)
    w_other = core_swap(w_mine)

    order = jnp.asarray(column_order(), jnp.int32)
    order = (order[:, None] == lax.broadcasted_iota(jnp.int32, (HD, HD), 1)).astype(BF16)

    flops = 2 * TILE * TILE * HD
    att, att_t, stats = call(
        forward_kernel,
        (meta, pos),
        (q, kl, k, kr, vl, v, vr, order),
        [(tile, BF16), ((GROUP, GROUP_ROWS, TILE), BF16), (small, F32)],
        6 * flops + 2 * TILE * HD * HD,
        8 * 1024 * 1024,
        HEADS * TILE * TILE * 3,
    )

    q2, og2, _, _, _, _ = lax.optimization_barrier((q, og, kl, kr, vl, vr))
    ql, qr = next_tile(q2, 1), next_tile(q2, -1)
    ogl, ogr = next_tile(og2, 1), next_tile(og2, -1)

    regrouped = lax.all_to_all(att_t, ("core", "x"), 0, 0, tiled=True)
    (partial,) = call(
        weight_kernel,
        (which,),
        (regrouped, og_mine, og_other),
        [((GROUP_ROWS, HD), BF16)],
        2 * TILE * HD * HD,
        4 * 1024 * 1024,
    )
    along_z = lax.all_to_all(partial.reshape(8, GROUP_ROWS // 8, HD), "z", 0, 0, tiled=True)
    sum_z = jnp.sum(along_z.astype(F32), axis=0)
    along_y = lax.all_to_all(sum_z.reshape(4, ROWS_OUT, HD), ("yhi", "ylo"), 0, 0, tiled=True)
    grad_weight = jnp.sum(along_y, axis=0)

    gal, gao, gar, stats = call(
        grad_attended_kernel,
        (which,),
        (w_mine, w_other, ogl, og, ogr, att, stats),
        [(tile, BF16), (tile, BF16), (tile, BF16), (small, F32)],
        6 * TILE * HD * HD,
        8 * 1024 * 1024,
    )
    stats_l, stats_r = next_tile(stats, 1), next_tile(stats, -1)
    (layer_out,) = call(
        project_kernel,
        (which,),
        (w_mine, w_other, att),
        [(tile, BF16)],
        2 * TILE * HD * HD,
        6 * 1024 * 1024,
    )
    dq, dk0, dv0 = call(
        row_kernel,
        (meta, pos),
        (q, kl, k, kr, vl, v, vr, gao, stats),
        [(tile, BF16), (tile, F32), (tile, F32)],
        11 * flops,
        6 * 1024 * 1024,
        HEADS * TILE * TILE * 3,
    )
    dk, dv = call(
        column_kernel,
        (meta, pos),
        (ql, qr, k, v, gal, gar, stats_l, stats_r, dk0, dv0),
        [(tile, BF16), (tile, BF16)],
        8 * flops,
        6 * 1024 * 1024,
        HEADS * TILE * TILE * 2,
    )
    return layer_out[None], dq[None], dk[None], dv[None], grad_weight


def solution(mesh):
    fine = jax.sharding.Mesh(np.asarray(mesh.devices).reshape(SIZES), NAMES)
    tokens = P(FSDP, FRAME, None)
    tiles = P(FSDP, FRAME)
    in_specs = (tokens, tokens, tokens, tiles, tiles, tiles, P(FSDP, None), tokens)
    out_specs = (tokens, tokens, tokens, tokens, P(FRAME + FSDP, None))
    return jax.shard_map(shards, mesh=fine, in_specs=in_specs, out_specs=out_specs, check_vma=False)
```

```python
import jax
import jax.numpy as jnp
import numpy as np
from jax import lax
from jax.experimental import pallas as pl
from jax.experimental.pallas import tpu as pltpu
from jax.sharding import PartitionSpec as P

HEADS = 12
HEAD_DIM = 128
TILE = 128
HD = HEADS * HEAD_DIM
SCALE = HEAD_DIM**-0.5
MASKED = -1e30

SIZES = (8, 2, 2, 2, 4)
NAMES = ("z", "yhi", "core", "ylo", "x")
FRAME = ("z", "yhi", "core")
FSDP = ("ylo", "x")
TILES = 32
ROWS_OUT = 6
GROUP = 8
GROUP_ROWS = HD // GROUP
EXTRA = 16

F32 = jnp.float32
BF16 = jnp.bfloat16
VMEM = pltpu.VMEM
NT = (((1,), (1,)), ((), ()))
NN = (((1,), (0,)), ((), ()))
TN = (((0,), (0,)), ((), ()))


def dot(a, b, dims=NN):
    return lax.dot_general(a, b, dims, preferred_element_type=F32)


def next_tile(value, step):
    return lax.ppermute(value, FRAME, [(i, (i + step) % TILES) for i in range(TILES)])


def core_swap(value):
    return lax.ppermute(value, "core", [(0, 1), (1, 0)])


def along_x(value, step):
    return lax.ppermute(value, "x", [((i + step) % 4, i) for i in range(4)])


def gather_x(value):
    spread = jnp.broadcast_to(value[None], (4,) + value.shape)
    return lax.all_to_all(spread, "x", 0, 0, tiled=True)


def after(value, *others):
    return lax.optimization_barrier((value, *others))[0]


def head(h):
    return slice(h * HEAD_DIM, (h + 1) * HEAD_DIM)


def visible(frame, low, high, there):
    seen = (frame >= low) & (frame <= high)
    return jnp.minimum(jnp.where(seen, 0.0, MASKED), jnp.where(there, 0.0, MASKED))


def told(tile):
    row = tile[2 * TILE : 2 * TILE + EXTRA, :HEAD_DIM].astype(F32)[:1]
    return row[:, 0:1], row[:, 1:2], row[:, 2:3]


def row_bias(info, left, right):
    frame, back, ahead = (info[n].astype(F32) for n in range(3))
    low, high, position = frame - back, frame + ahead, info[3]
    place = lax.broadcasted_iota(jnp.int32, (1, 3 * TILE), 1)
    on_left = visible(told(left)[0], low, high, position > 0)
    on_right = visible(told(right)[0], low, high, position < TILES - 1)
    return jnp.where(place < TILE, on_left, jnp.where(place < 2 * TILE, 0.0, on_right))


def column_bias(info, left, right):
    frame, position = info[0].astype(F32), info[3]
    place = lax.broadcasted_iota(jnp.int32, (1, 2 * TILE), 1)
    sides = []
    for tile, there in ((left, position > 0), (right, position < TILES - 1)):
        center, back, ahead = told(tile)
        sides.append(visible(frame, center - back, center + ahead, there))
    return jnp.where(place < TILE, sides[0], sides[1])


KEYS = slice(0, TILE)
VALUES = slice(TILE, 2 * TILE)


def forward_kernel(scalars, near, far, copies, outs, scratch):
    (info,) = scalars
    q, k, v, left, right = near
    (order,) = far
    att, att_t, stats = outs
    lane = lax.broadcasted_iota(jnp.int32, (TILE, 128), 1)
    total = jnp.zeros((TILE, 128), F32)
    for h in range(HEADS):
        if h == 0:
            bias = row_bias(info, left, right)
        c = head(h)
        keys = jnp.concatenate([left[KEYS, c], k[:, c], right[KEYS, c]], axis=0)
        values = jnp.concatenate([left[VALUES, c], v[:, c], right[VALUES, c]], axis=0)
        s = dot(q[:, c], keys, NT) * SCALE + bias
        top = jnp.max(s, axis=1, keepdims=True)
        e = jnp.exp(s - top)
        mass = jnp.sum(e, axis=1, keepdims=True)
        p = (e * (1.0 / mass)).astype(BF16)
        att[:, c] = dot(p, values).astype(BF16)
        total = jnp.where(lane == h, top + jnp.log(mass), total)
    stats[...] = total
    copies[0].wait()
    for g in range(GROUP):
        cols = slice(g * GROUP_ROWS, (g + 1) * GROUP_ROWS)
        att_t[g] = dot(order[cols, :], att[...], NT).astype(BF16)


def place(info, n):
    side, step = divmod(n, 4)
    core = info[4] if side == 0 else 1 - info[4]
    return core * 4 + lax.rem(info[5] + step, 4)


def spread_kernel(scalars, near, far, copies, outs, scratch):
    (info,), (out, w) = scalars, outs
    att_t, held, passed, *grads = near
    out[:, :GROUP_ROWS, :] = att_t[...]
    w[...] = jnp.where(info[4] == info[7], held[...], passed[...])
    for side in range(2):
        core = info[4] if side == 0 else 1 - info[4]
        for n in range(0, 4, 2):
            pair = grads[side][n : n + 2].reshape(2 * TILE, HD)
            got = dot(w[...], pair, NT).astype(BF16)
            out[core * 4 + n, GROUP_ROWS:, :] = got[:, :TILE]
            out[core * 4 + n + 1, GROUP_ROWS:, :] = got[:, TILE:]


def weight_kernel(scalars, near, far, copies, outs, scratch):
    (info,), (mixed, *grads), (out,) = scalars, near, outs
    acc = None
    for side in range(2):
        core = info[4] if side == 0 else 1 - info[4]
        left = jnp.concatenate([mixed[core * 4 + n, :GROUP_ROWS, :] for n in range(4)], axis=1)
        term = dot(left, grads[side][...].reshape(4 * TILE, HD))
        acc = term if acc is None else acc + term
    out[...] = (acc * float(GROUP * TILES * TILE) ** -0.5).astype(BF16)


def delta_kernel(scalars, near, far, copies, outs, scratch):
    mixed, att, stats = near
    ga, out = outs
    lane = lax.broadcasted_iota(jnp.int32, (TILE, 128), 1)
    total = stats[...]
    rows = mixed[:, GROUP_ROWS:, :].reshape(HD, TILE)
    for h in range(HEADS):
        c = head(h)
        own = rows[c, :].T
        ga[:TILE, c] = own
        terms = own.astype(F32) * att[:, c].astype(F32)
        total = jnp.where(lane == HEADS + h, jnp.sum(terms, axis=1, keepdims=True), total)
    out[...] = total
    turned = total.T
    rest = [
        jnp.concatenate([turned[k * HEADS + h : k * HEADS + h + 1, :] for h in range(HEADS)], axis=1)
        for k in range(2)
    ]
    terms = []
    for _ in range(3):
        for k in range(2):
            part = rest[k].astype(BF16).astype(F32)
            rest[k] = rest[k] - part
            terms.append(part)
    terms.append(jnp.zeros((EXTRA - len(terms), HD), F32))
    ga[TILE:, :] = jnp.concatenate(terms, axis=0).astype(BF16)


def sum_kernel(scalars, near, far, copies, outs, scratch):
    (info,), (parts,) = scalars, near
    total = parts[0].astype(F32)
    for n in range(1, 8):
        total += parts[n].astype(F32)
    pieces = [total[n * ROWS_OUT : (n + 1) * ROWS_OUT, :] for n in range(4)]
    for step, ref in enumerate(outs):
        want = jnp.bitwise_xor(info[6], step)
        low = jnp.where(want == 0, pieces[0], pieces[1])
        high = jnp.where(want == 2, pieces[2], pieces[3])
        ref[...] = jnp.where(want < 2, low, high)


def project_kernel(scalars, near, far, copies, outs, scratch):
    (info,), (att,), (out,), (turned,) = scalars, near, outs, scratch
    for h in range(HEADS):
        turned[head(h), :] = att[:, head(h)].T
    acc = jnp.zeros((TILE, HD), F32)
    for n in range(GROUP):
        copies[n].wait()
        first = pl.multiple_of(place(info, n) * GROUP_ROWS, GROUP_ROWS)
        acc += dot(turned[pl.ds(first, GROUP_ROWS), :], far[n][...], TN)
    out[...] = acc.astype(BF16)


def backward_kernel(scalars, near, far, copies, outs, scratch):
    (info,), (dq, dk, dv) = scalars, outs
    stats, q, k, v, left, right, ga, ql, qr, gal, gar = near
    st = stats[...]
    for h in range(HEADS):
        if h == 0:
            on_row, on_column = row_bias(info, left, right), column_bias(info, left, right)
        c = head(h)
        keys = jnp.concatenate([left[KEYS, c], k[:, c], right[KEYS, c]], axis=0)
        values = jnp.concatenate([left[VALUES, c], v[:, c], right[VALUES, c]], axis=0)
        qh, gh = q[:, c], ga[:TILE, c]
        s = dot(qh, keys, NT) * SCALE + on_row
        p = jnp.exp(s - st[:, h : h + 1])
        dp = dot(gh, values, NT)
        ds = (p * (dp - st[:, HEADS + h : HEADS + h + 1]) * SCALE).astype(BF16)
        dq[:, c] = dot(ds, keys).astype(BF16)
        dkh = dot(ds[:, TILE : 2 * TILE], qh, TN)
        dvh = dot(p[:, TILE : 2 * TILE].astype(BF16), gh, TN)

        queries = jnp.concatenate([ql[:, c], qr[:, c]], axis=0)
        grads = jnp.concatenate([gal[:TILE, c], gar[:TILE, c]], axis=0)
        sent = [g[TILE:, c].astype(F32) for g in (gal, gar)]
        lse, delta = (
            jnp.concatenate([t[n : n + 1] + t[n + 2 : n + 3] + t[n + 4 : n + 5] for t in sent], axis=1)
            for n in range(2)
        )
        s = dot(k[:, c], queries, NT) * SCALE + on_column
        p = jnp.exp(s - lse)
        dp = dot(v[:, c], grads, NT)
        ds = (p * (dp - delta) * SCALE).astype(BF16)
        dk[:, c] = (dkh + dot(ds, queries)).astype(BF16)
        dv[:, c] = (dvh + dot(p.astype(BF16), grads)).astype(BF16)


def call(kernel, micros, scalars, near, far, outs, scratch=(), mib=4):
    counts = [len(scalars), len(near), len(far), len(outs), len(far), len(scratch)]
    ends = np.cumsum(counts)

    def body(*refs):
        parts = [refs[end - count : end] for end, count in zip(ends, counts)]
        sems = refs[ends[-1]]
        copies = [
            pltpu.make_async_copy(ref, buffer, sems.at[n])
            for n, (ref, buffer) in enumerate(zip(parts[2], parts[4]))
        ]
        for copy in copies:
            copy.start()
        kernel(parts[0], parts[1], parts[4], copies, parts[3], parts[5])

    return pl.pallas_call(
        body,
        in_specs=[pl.BlockSpec(memory_space=pltpu.SMEM)] * len(scalars)
        + [pl.BlockSpec(memory_space=VMEM)] * len(near)
        + [pl.BlockSpec(memory_space=pl.ANY)] * len(far),
        out_specs=[pl.BlockSpec(memory_space=VMEM)] * len(outs),
        out_shape=[jax.ShapeDtypeStruct(s, d) for s, d in outs],
        scratch_shapes=[VMEM(f.shape, f.dtype) for f in far]
        + [VMEM(s, d) for s, d in scratch]
        + [pltpu.SemaphoreType.DMA((max(1, len(far)),))],
        cost_estimate=pl.CostEstimate(flops=int(micros * 1e9), bytes_accessed=1024, transcendentals=0),
        compiler_params=pltpu.CompilerParams(vmem_limit_bytes=mib * 1024 * 1024),
    )(*scalars, *near, *far)


def column_order():
    features = np.arange(HD).reshape(SIZES + (ROWS_OUT,))
    return features.transpose(2, 4, 0, 1, 3, 5).reshape(-1)


def shards(query_rows, key_rows, value_rows, frame_of, reach_back, reach_ahead, out_weight, out_grad):
    core = lax.axis_index("core")
    q, k, v, og = query_rows[0], key_rows[0], value_rows[0], out_grad[0]
    tile = (TILE, HD)
    where = (lax.axis_index(FRAME), core, lax.axis_index("x"), lax.axis_index(("yhi", "ylo")))
    where = where + (lax.axis_index("ylo"),)
    info = jnp.stack([frame_of[0, 0], reach_back[0, 0], reach_ahead[0, 0], *where]).astype(jnp.int32)

    note = jnp.pad(info[None, :3].astype(BF16), ((0, EXTRA - 1), (0, HD - 3)))
    to_send = jnp.concatenate([k, v, note], axis=0)
    left, right = next_tile(to_send, 1), next_tile(to_send, -1)

    og_mine = gather_x(after(og, to_send))
    og_other = core_swap(og_mine)

    w_passed = lax.ppermute(after(out_weight, left, right), ("core", "ylo"), [(0, 1), (3, 2)])

    q2 = after(q, left, right)
    ql, qr = next_tile(q2, 1), next_tile(q2, -1)

    order = jnp.asarray(np.eye(HD, dtype=np.float32)[column_order()], BF16)
    att, att_t, stats = call(
        forward_kernel,
        8,
        (info,),
        (q, k, v, left, right),
        (order,),
        [(tile, BF16), ((GROUP, GROUP_ROWS, TILE), BF16), ((TILE, 128), F32)],
        mib=16,
    )

    mixed, w_block = call(
        spread_kernel,
        2,
        (info,),
        (after(att_t, ql, qr), out_weight, w_passed, og_mine, og_other),
        (),
        [((GROUP, 2 * GROUP_ROWS, TILE), BF16), ((GROUP_ROWS, HD), BF16)],
    )
    mixed = lax.all_to_all(mixed, ("core", "x"), 0, 0, tiled=True)

    ga, stats = call(
        delta_kernel,
        1,
        (),
        (mixed, att, stats),
        (),
        [((TILE + EXTRA, HD), BF16), ((TILE, 128), F32)],
    )
    gal, gar = next_tile(ga, 1), next_tile(ga, -1)

    w_late = after(w_block, ga)
    blocks = [w_block] + [along_x(w_late, step) for step in (1, 2, 3)]

    (partial,) = call(
        weight_kernel,
        2,
        (info,),
        (after(mixed, ga), og_mine, og_other),
        (),
        [((GROUP_ROWS, HD), BF16)],
    )
    along_z = lax.all_to_all(partial.reshape(8, GROUP_ROWS // 8, HD), "z", 0, 0, tiled=True)

    dq, dk, dv = call(
        backward_kernel,
        9,
        (info,),
        (after(stats, partial), q, k, v, left, right, ga, ql, qr, gal, gar),
        (),
        [(tile, BF16)] * 3,
        mib=8,
    )

    pieces = call(
        sum_kernel,
        1,
        (info,),
        (after(along_z, dq),),
        (),
        [((ROWS_OUT, HD), F32)] * 4,
    )
    arrived = []
    for step in (1, 2, 3):
        pairs = [(i, i ^ step) for i in range(4)]
        arrived.append(lax.ppermute(pieces[step], ("yhi", "ylo"), pairs))

    blocks = blocks + [core_swap(after(w, dq)) for w in blocks]
    (layer_out,) = call(
        project_kernel,
        4,
        (info,),
        (after(att, pieces[0]),),
        tuple(blocks),
        [(tile, BF16)],
        scratch=[((HD, TILE), BF16)],
        mib=16,
    )
    grad_weight = after(pieces[0], layer_out) + arrived[0] + arrived[1] + arrived[2]
    return layer_out[None], dq[None], dk[None], dv[None], grad_weight


def solution(mesh):
    fine = jax.sharding.Mesh(np.asarray(mesh.devices).reshape(SIZES), NAMES)
    tokens = P(FSDP, FRAME, None)
    tiles = P(FSDP, FRAME)
    in_specs = (tokens, tokens, tokens, tiles, tiles, tiles, P(FSDP, None), tokens)
    out_specs = (tokens, tokens, tokens, tokens, P(FRAME + FSDP, None))
    return jax.shard_map(shards, mesh=fine, in_specs=in_specs, out_specs=out_specs, check_vma=False)
```

```python
import jax
import jax.numpy as jnp
import numpy as np
from jax import lax
from jax.experimental import pallas as pl
from jax.experimental.pallas import tpu as pltpu
from jax.sharding import PartitionSpec as P

HEADS = 12
HEAD_DIM = 128
TILE = 128
HD = HEADS * HEAD_DIM
SCALE = HEAD_DIM**-0.5
MASKED = -1e30

SIZES = (8, 2, 2, 2, 4)
NAMES = ("z", "yhi", "core", "ylo", "x")
FRAME = ("z", "yhi", "core")
FSDP = ("ylo", "x")
TILES = 32
ROWS_OUT = 6
GROUP = 8
GROUP_ROWS = HD // GROUP
EXTRA = 16
SPAN = 384
CHUNKS = 4

F32 = jnp.float32
BF16 = jnp.bfloat16
VMEM = pltpu.VMEM
NT = (((1,), (1,)), ((), ()))
NN = (((1,), (0,)), ((), ()))
TN = (((0,), (0,)), ((), ()))


def dot(a, b, dims=NN):
    return lax.dot_general(a, b, dims, preferred_element_type=F32)


def next_tile(value, step):
    return lax.ppermute(value, FRAME, [(i, (i + step) % TILES) for i in range(TILES)])


def core_swap(value):
    return lax.ppermute(value, "core", [(0, 1), (1, 0)])


def along_x(value, step):
    return lax.ppermute(value, "x", [((i + step) % 4, i) for i in range(4)])


def along_x(value, step):
    return lax.ppermute(value, "x", [((i + step) % 4, i) for i in range(4)])


def after(value, *others):
    return lax.optimization_barrier((value, *others))[0]


def head(h):
    return slice(h * HEAD_DIM, (h + 1) * HEAD_DIM)


def visible(frame, low, high, there):
    seen = (frame >= low) & (frame <= high)
    return jnp.minimum(jnp.where(seen, 0.0, MASKED), jnp.where(there, 0.0, MASKED))


def told(tile):
    row = tile[2 * TILE : 2 * TILE + EXTRA, :HEAD_DIM].astype(F32)[:1]
    return row[:, 0:1], row[:, 1:2], row[:, 2:3]


def row_bias(info, left, right):
    frame, back, ahead = (info[n].astype(F32) for n in range(3))
    low, high, position = frame - back, frame + ahead, info[3]
    column = lax.broadcasted_iota(jnp.int32, (1, 3 * TILE), 1)
    on_left = visible(told(left)[0], low, high, position > 0)
    on_right = visible(told(right)[0], low, high, position < TILES - 1)
    return jnp.where(column < TILE, on_left, jnp.where(column < 2 * TILE, 0.0, on_right))


def column_bias(info, left, right):
    frame, position = info[0].astype(F32), info[3]
    column = lax.broadcasted_iota(jnp.int32, (1, 2 * TILE), 1)
    sides = []
    for tile, there in ((left, position > 0), (right, position < TILES - 1)):
        center, back, ahead = told(tile)
        sides.append(visible(frame, center - back, center + ahead, there))
    return jnp.where(column < TILE, sides[0], sides[1])


KEYS = slice(0, TILE)
VALUES = slice(TILE, 2 * TILE)


def pack_kernel(frame, back, ahead, k, v, out, sems):
    copies = [
        pltpu.make_async_copy(k, out.at[KEYS], sems.at[0]),
        pltpu.make_async_copy(v, out.at[VALUES], sems.at[1]),
    ]
    for copy in copies:
        copy.start()
    lane = lax.broadcasted_iota(jnp.int32, (EXTRA, HD), 1)
    said = jnp.where(lane == 0, frame[0, 0], jnp.where(lane == 1, back[0, 0], ahead[0, 0]))
    out[2 * TILE :, :] = said.astype(F32).astype(BF16)
    for copy in copies:
        copy.wait()


def pack(frame, back, ahead, k, v):
    return pl.pallas_call(
        pack_kernel,
        in_specs=[pl.BlockSpec(memory_space=pltpu.SMEM)] * 3 + [pl.BlockSpec(memory_space=pltpu.HBM)] * 2,
        out_specs=pl.BlockSpec(memory_space=VMEM),
        out_shape=jax.ShapeDtypeStruct((2 * TILE + EXTRA, HD), BF16),
        scratch_shapes=[pltpu.SemaphoreType.DMA((2,))],
        compiler_params=pltpu.CompilerParams(vmem_limit_bytes=56 * 1024 * 1024),
    )(frame, back, ahead, k, v)


def join_kernel(*refs):
    parts, out, sems = refs[:-2], refs[-2], refs[-1]
    copies = [
        pltpu.make_async_copy(part, out.at[n * TILE : (n + 1) * TILE], sems.at[n])
        for n, part in enumerate(parts)
    ]
    for copy in copies:
        copy.start()
    for copy in copies:
        copy.wait()


def join(parts):
    return pl.pallas_call(
        join_kernel,
        in_specs=[pl.BlockSpec(memory_space=pltpu.HBM)] * len(parts),
        out_specs=pl.BlockSpec(memory_space=VMEM),
        out_shape=jax.ShapeDtypeStruct((len(parts) * TILE, HD), BF16),
        scratch_shapes=[pltpu.SemaphoreType.DMA((len(parts),))],
        cost_estimate=pl.CostEstimate(flops=1024, bytes_accessed=1024, transcendentals=0),
        compiler_params=pltpu.CompilerParams(vmem_limit_bytes=4 * 1024 * 1024),
    )(*parts)


def forward_kernel(scalars, near, far, copies, outs, scratch):
    (info,) = scalars
    q, k, v, left, right, order = near
    att, att_t, stats = outs
    bias = row_bias(info, left, right)
    lane = lax.broadcasted_iota(jnp.int32, (TILE, 128), 1)
    total = jnp.zeros((TILE, 128), F32)
    for h in range(HEADS):
        c = head(h)
        keys = jnp.concatenate([left[KEYS, c], k[:, c], right[KEYS, c]], axis=0)
        values = jnp.concatenate([left[VALUES, c], v[:, c], right[VALUES, c]], axis=0)
        s = dot(q[:, c], keys, NT) * SCALE + bias
        top = jnp.max(s, axis=1, keepdims=True)
        e = jnp.exp(s - top)
        mass = jnp.sum(e, axis=1, keepdims=True)
        p = (e * (1.0 / mass)).astype(BF16)
        att[:, c] = dot(p, values).astype(BF16)
        total = jnp.where(lane == h, top + jnp.log(mass), total)
        if (h + 1) * HEAD_DIM % SPAN == 0:
            n = (h + 1) * HEAD_DIM // SPAN - 1
            moved = dot(order[...], att[:, n * SPAN : (n + 1) * SPAN], NT).astype(BF16)
            rows = SPAN // GROUP
            for g in range(GROUP):
                att_t[g, n * rows : (n + 1) * rows, :] = moved[g * rows : (g + 1) * rows]
    stats[...] = total


def place(info, n):
    side, step = divmod(n, 4)
    core = info[4] if side == 0 else 1 - info[4]
    return core * 4 + lax.rem(info[5] + step, 4)


def spread_kernel(scalars, near, far, copies, outs, scratch):
    (info,), (out, w) = scalars, outs
    att_t, held, passed, *grads = near
    out[:, :GROUP_ROWS, :] = att_t[...]
    w[...] = jnp.where(info[4] == info[7], held[...], passed[...])
    for side in range(2):
        for n in range(0, 4, 2):
            pair = grads[side][n * TILE : (n + 2) * TILE, :]
            got = dot(w[...], pair, NT).astype(BF16)
            out[place(info, side * 4 + n), GROUP_ROWS:, :] = got[:, :TILE]
            out[place(info, side * 4 + n + 1), GROUP_ROWS:, :] = got[:, TILE:]


def weight_kernel(scalars, near, far, copies, outs, scratch):
    (info,), (mixed, *grads), (out,) = scalars, near, outs
    acc = None
    for side in range(2):
        rows = [mixed[place(info, side * 4 + n), :GROUP_ROWS, :] for n in range(4)]
        term = dot(jnp.concatenate(rows, axis=1), grads[side][...])
        acc = term if acc is None else acc + term
    out[...] = (acc * float(GROUP * TILES * TILE) ** -0.5).astype(BF16)


def delta_kernel(scalars, near, far, copies, outs, scratch):
    mixed, att, stats = near
    ga, out = outs
    lane = lax.broadcasted_iota(jnp.int32, (TILE, 128), 1)
    total = stats[...]
    rows = mixed[:, GROUP_ROWS:, :].reshape(HD, TILE)
    for h in range(HEADS):
        c = head(h)
        own = rows[c, :].T
        ga[:TILE, c] = own
        terms = own.astype(F32) * att[:, c].astype(F32)
        total = jnp.where(lane == HEADS + h, jnp.sum(terms, axis=1, keepdims=True), total)
    out[...] = total
    turned = total.T
    rest = [
        jnp.concatenate([turned[k * HEADS + h : k * HEADS + h + 1, :] for h in range(HEADS)], axis=1)
        for k in range(2)
    ]
    terms = []
    for _ in range(3):
        for k in range(2):
            part = rest[k].astype(BF16).astype(F32)
            rest[k] = rest[k] - part
            terms.append(part)
    terms.append(jnp.zeros((EXTRA - len(terms), HD), F32))
    ga[TILE:, :] = jnp.concatenate(terms, axis=0).astype(BF16)


def sum_kernel(scalars, near, far, copies, outs, scratch):
    (info,), (parts,) = scalars, near
    total = parts[0].astype(F32)
    for n in range(1, 8):
        total += parts[n].astype(F32)
    pieces = [total[n * ROWS_OUT : (n + 1) * ROWS_OUT, :] for n in range(4)]
    for step, ref in enumerate(outs):
        want = jnp.bitwise_xor(info[6], step)
        low = jnp.where(want == 0, pieces[0], pieces[1])
        high = jnp.where(want == 2, pieces[2], pieces[3])
        ref[...] = jnp.where(want < 2, low, high)


def project_kernel(scalars, near, far, copies, outs, scratch):
    (info,), (att, *blocks), (out,), (turned,) = scalars, near, outs, scratch
    for h in range(HEADS):
        turned[head(h), :] = att[:, head(h)].T
    acc = jnp.zeros((TILE, HD), F32)
    for n in range(GROUP):
        first = pl.multiple_of(place(info, n) * GROUP_ROWS, GROUP_ROWS)
        acc += dot(turned[pl.ds(first, GROUP_ROWS), :], blocks[n][...], TN)
    out[...] = acc.astype(BF16)


def backward_kernel(scalars, near, far, copies, outs, scratch):
    dq, dk, dv = outs
    (info,), (stats,) = scalars, near
    q, k, v, left, right, ga, ql, qr, gal, gar = far
    st = stats[...]
    for h in range(HEADS):
        if h % (HEADS // CHUNKS) == 0:
            for copy in copies[h // (HEADS // CHUNKS)]:
                copy.wait()
        if h == 0:
            on_row, on_column = row_bias(info, left, right), column_bias(info, left, right)
        c = head(h)
        keys = jnp.concatenate([left[KEYS, c], k[:, c], right[KEYS, c]], axis=0)
        values = jnp.concatenate([left[VALUES, c], v[:, c], right[VALUES, c]], axis=0)
        qh, gh = q[:, c], ga[:TILE, c]
        s = dot(qh, keys, NT) * SCALE + on_row
        p = jnp.exp(s - st[:, h : h + 1])
        dp = dot(gh, values, NT)
        ds = (p * (dp - st[:, HEADS + h : HEADS + h + 1]) * SCALE).astype(BF16)
        dq[:, c] = dot(ds, keys).astype(BF16)
        dkh = dot(ds[:, TILE : 2 * TILE], qh, TN)
        dvh = dot(p[:, TILE : 2 * TILE].astype(BF16), gh, TN)

        queries = jnp.concatenate([ql[:, c], qr[:, c]], axis=0)
        grads = jnp.concatenate([gal[:TILE, c], gar[:TILE, c]], axis=0)
        sent = [g[TILE:, c].astype(F32) for g in (gal, gar)]
        lse, delta = (
            jnp.concatenate([t[n : n + 1] + t[n + 2 : n + 3] + t[n + 4 : n + 5] for t in sent], axis=1)
            for n in range(2)
        )
        s = dot(k[:, c], queries, NT) * SCALE + on_column
        p = jnp.exp(s - lse)
        dp = dot(v[:, c], grads, NT)
        ds = (p * (dp - delta) * SCALE).astype(BF16)
        dk[:, c] = (dkh + dot(ds, queries)).astype(BF16)
        dv[:, c] = (dvh + dot(p.astype(BF16), grads)).astype(BF16)


def call(kernel, micros, scalars, near, far, outs, scratch=(), mib=4, chunks=1):
    counts = [len(scalars), len(near), len(far), len(outs), len(far), len(scratch)]
    ends = np.cumsum(counts)

    def body(*refs):
        parts = [refs[end - count : end] for end, count in zip(ends, counts)]
        sems = refs[ends[-1]]
        copies = [[] for _ in range(chunks)]
        for chunk in range(chunks):
            for n, (ref, buffer) in enumerate(zip(parts[2], parts[4])):
                width = buffer.shape[-1] // chunks
                cols = (slice(None),) * (len(buffer.shape) - 1) + (pl.ds(chunk * width, width),)
                copy = pltpu.make_async_copy(ref.at[cols], buffer.at[cols], sems.at[n, chunk])
                copy.start()
                copies[chunk].append(copy)
        kernel(parts[0], parts[1], parts[4], copies if chunks > 1 else copies[0], parts[3], parts[5])

    return pl.pallas_call(
        body,
        in_specs=[pl.BlockSpec(memory_space=pltpu.SMEM)] * len(scalars)
        + [pl.BlockSpec(memory_space=VMEM)] * len(near)
        + [pl.BlockSpec(memory_space=pltpu.HBM)] * len(far),
        out_specs=[pl.BlockSpec(memory_space=VMEM)] * len(outs),
        out_shape=[jax.ShapeDtypeStruct(s, d) for s, d in outs],
        scratch_shapes=[VMEM(f.shape, f.dtype) for f in far]
        + [VMEM(s, d) for s, d in scratch]
        + [pltpu.SemaphoreType.DMA((max(1, len(far)), chunks))],
        cost_estimate=pl.CostEstimate(flops=int(micros * 1e9), bytes_accessed=1024, transcendentals=0),
        compiler_params=pltpu.CompilerParams(vmem_limit_bytes=mib * 1024 * 1024),
    )(*scalars, *near, *far)


def column_order():
    features = np.arange(SPAN).reshape(SPAN // 96, 2, 2, 4, ROWS_OUT)
    return np.eye(SPAN, dtype=np.float32)[features.transpose(1, 3, 0, 2, 4).reshape(-1)]


def shards(query_rows, key_rows, value_rows, frame_of, reach_back, reach_ahead, out_weight, out_grad):
    core = lax.axis_index("core")
    q, k, v, og = query_rows[0], key_rows[0], value_rows[0], out_grad[0]
    tile = (TILE, HD)
    where = (lax.axis_index(FRAME), core, lax.axis_index("x"), lax.axis_index(("yhi", "ylo")))
    where = where + (lax.axis_index("ylo"),)
    info = jnp.stack([frame_of[0, 0], reach_back[0, 0], reach_ahead[0, 0], *where]).astype(jnp.int32)

    to_send = pack(frame_of, reach_back, reach_ahead, k, v)
    left, right = next_tile(to_send, 1), next_tile(to_send, -1)

    w_passed = lax.ppermute(out_weight, ("core", "ylo"), [(0, 1), (3, 2)])

    og_sent = after(og, to_send)
    og_mine = join([og] + [along_x(og_sent, step) for step in (1, 2, 3)])
    og_other = core_swap(og_mine)

    order = jnp.asarray(column_order(), BF16)
    att, att_t, stats = call(
        forward_kernel,
        8,
        (info,),
        (q, k, v, left, right, order),
        (),
        [(tile, BF16), ((GROUP, GROUP_ROWS, TILE), BF16), ((TILE, 128), F32)],
        mib=8,
    )

    q2 = after(q, att)
    ql, qr = next_tile(q2, 1), next_tile(q2, -1)

    mixed, w_block = call(
        spread_kernel,
        2,
        (info,),
        (att_t, out_weight, w_passed, og_mine, og_other),
        (),
        [((GROUP, 2 * GROUP_ROWS, TILE), BF16), ((GROUP_ROWS, HD), BF16)],
    )
    blocks = [w_block] + [along_x(w_block, step) for step in (1, 2, 3)]
    mixed = lax.all_to_all(mixed, ("core", "x"), 0, 0, tiled=True)

    ga, stats = call(
        delta_kernel,
        1,
        (),
        (after(mixed, ql, qr), att, stats),
        (),
        [((TILE + EXTRA, HD), BF16), ((TILE, 128), F32)],
    )
    gal, gar = next_tile(ga, 1), next_tile(ga, -1)

    (partial,) = call(
        weight_kernel,
        2,
        (info,),
        (after(mixed, ga), og_mine, og_other),
        (),
        [((GROUP_ROWS, HD), BF16)],
    )
    along_z = lax.all_to_all(partial.reshape(8, GROUP_ROWS // 8, HD), "z", 0, 0, tiled=True)

    dq, dk, dv = call(
        backward_kernel,
        9,
        (info,),
        (after(stats, partial, blocks[1], blocks[3]),),
        (q, k, v, left, right, ga, ql, qr, gal, gar),
        [(tile, BF16)] * 3,
        mib=56,
        chunks=CHUNKS,
    )
    blocks = blocks + [core_swap(after(w, dq)) for w in blocks]

    pieces = call(
        sum_kernel,
        1,
        (info,),
        (after(along_z, dq),),
        (),
        [((ROWS_OUT, HD), F32)] * 4,
    )
    arrived = []
    for step in (1, 2, 3):
        pairs = [(i, i ^ step) for i in range(4)]
        arrived.append(lax.ppermute(pieces[step], ("yhi", "ylo"), pairs))

    (layer_out,) = call(
        project_kernel,
        4,
        (info,),
        (after(att, pieces[0]), *blocks),
        (),
        [(tile, BF16)],
        scratch=[((HD, TILE), BF16)],
    )
    grad_weight = after(pieces[0], layer_out) + arrived[0] + arrived[1] + arrived[2]
    return layer_out[None], dq[None], dk[None], dv[None], grad_weight


def solution(mesh):
    fine = jax.sharding.Mesh(np.asarray(mesh.devices).reshape(SIZES), NAMES)
    tokens = P(FSDP, FRAME, None)
    tiles = P(FSDP, FRAME)
    in_specs = (tokens, tokens, tokens, tiles, tiles, tiles, P(FSDP, None), tokens)
    out_specs = (tokens, tokens, tokens, tokens, P(FRAME + FSDP, None))
    return jax.shard_map(shards, mesh=fine, in_specs=in_specs, out_specs=out_specs, check_vma=False)
```

```python
import jax
import jax.numpy as jnp
import numpy as np
from jax import lax
from jax.experimental import pallas as pl
from jax.experimental.pallas import tpu as pltpu
from jax.sharding import PartitionSpec as P

HEADS = 12
HEAD_DIM = 128
TILE = 128
HD = HEADS * HEAD_DIM
SCALE = HEAD_DIM**-0.5
MASKED = -1e30

SIZES = (8, 2, 2, 2, 4)
NAMES = ("z", "yhi", "core", "ylo", "x")
FRAME = ("z", "yhi", "core")
FSDP = ("ylo", "x")
TILES = 32
ROWS_OUT = 6
GROUP = 8
GROUP_ROWS = HD // GROUP
EXTRA = 16
SPAN = 384
CHUNKS = 4

F32 = jnp.float32
BF16 = jnp.bfloat16
VMEM = pltpu.VMEM
NT = (((1,), (1,)), ((), ()))
NN = (((1,), (0,)), ((), ()))
TN = (((0,), (0,)), ((), ()))


def dot(a, b, dims=NN):
    return lax.dot_general(a, b, dims, preferred_element_type=F32)


def next_tile(value, step):
    return lax.ppermute(value, FRAME, [(i, (i + step) % TILES) for i in range(TILES)])


def core_swap(value):
    return lax.ppermute(value, "core", [(0, 1), (1, 0)])


def along_x(value, step):
    return lax.ppermute(value, "x", [((i + step) % 4, i) for i in range(4)])


def along_x(value, step):
    return lax.ppermute(value, "x", [((i + step) % 4, i) for i in range(4)])


def after(value, *others):
    return lax.optimization_barrier((value, *others))[0]


def head(h):
    return slice(h * HEAD_DIM, (h + 1) * HEAD_DIM)


def visible(frame, low, high, there):
    seen = (frame >= low) & (frame <= high)
    return jnp.minimum(jnp.where(seen, 0.0, MASKED), jnp.where(there, 0.0, MASKED))


def told(tile):
    row = tile[2 * TILE : 2 * TILE + EXTRA, :HEAD_DIM].astype(F32)[:1]
    return row[:, 0:1], row[:, 1:2], row[:, 2:3]


def row_bias(info, left, right):
    frame, back, ahead = (info[n].astype(F32) for n in range(3))
    low, high, position = frame - back, frame + ahead, info[3]
    column = lax.broadcasted_iota(jnp.int32, (1, 3 * TILE), 1)
    on_left = visible(told(left)[0], low, high, position > 0)
    on_right = visible(told(right)[0], low, high, position < TILES - 1)
    return jnp.where(column < TILE, on_left, jnp.where(column < 2 * TILE, 0.0, on_right))


def column_bias(info, left, right):
    frame, position = info[0].astype(F32), info[3]
    column = lax.broadcasted_iota(jnp.int32, (1, 2 * TILE), 1)
    sides = []
    for tile, there in ((left, position > 0), (right, position < TILES - 1)):
        center, back, ahead = told(tile)
        sides.append(visible(frame, center - back, center + ahead, there))
    return jnp.where(column < TILE, sides[0], sides[1])


KEYS = slice(0, TILE)
VALUES = slice(TILE, 2 * TILE)


def pack_kernel(frame, back, ahead, k, v, out, sems):
    copies = [
        pltpu.make_async_copy(k, out.at[KEYS], sems.at[0]),
        pltpu.make_async_copy(v, out.at[VALUES], sems.at[1]),
    ]
    for copy in copies:
        copy.start()
    lane = lax.broadcasted_iota(jnp.int32, (EXTRA, HD), 1)
    said = jnp.where(lane == 0, frame[0, 0], jnp.where(lane == 1, back[0, 0], ahead[0, 0]))
    out[2 * TILE :, :] = said.astype(F32).astype(BF16)
    for copy in copies:
        copy.wait()


def pack(frame, back, ahead, k, v):
    return pl.pallas_call(
        pack_kernel,
        in_specs=[pl.BlockSpec(memory_space=pltpu.SMEM)] * 3 + [pl.BlockSpec(memory_space=pltpu.HBM)] * 2,
        out_specs=pl.BlockSpec(memory_space=VMEM),
        out_shape=jax.ShapeDtypeStruct((2 * TILE + EXTRA, HD), BF16),
        scratch_shapes=[pltpu.SemaphoreType.DMA((2,))],
        compiler_params=pltpu.CompilerParams(vmem_limit_bytes=56 * 1024 * 1024),
    )(frame, back, ahead, k, v)


def join_kernel(*refs):
    parts, out, sems = refs[:-2], refs[-2], refs[-1]
    copies = [
        pltpu.make_async_copy(part, out.at[n * TILE : (n + 1) * TILE], sems.at[n])
        for n, part in enumerate(parts)
    ]
    for copy in copies:
        copy.start()
    for copy in copies:
        copy.wait()


def join(parts):
    return pl.pallas_call(
        join_kernel,
        in_specs=[pl.BlockSpec(memory_space=pltpu.HBM)] * len(parts),
        out_specs=pl.BlockSpec(memory_space=VMEM),
        out_shape=jax.ShapeDtypeStruct((len(parts) * TILE, HD), BF16),
        scratch_shapes=[pltpu.SemaphoreType.DMA((len(parts),))],
        cost_estimate=pl.CostEstimate(flops=1024, bytes_accessed=1024, transcendentals=0),
        compiler_params=pltpu.CompilerParams(vmem_limit_bytes=4 * 1024 * 1024),
    )(*parts)


def forward_kernel(scalars, near, far, copies, outs, scratch):
    (info,) = scalars
    q, k, v, left, right, order = near
    att, att_t, stats = outs
    bias = row_bias(info, left, right)
    lane = lax.broadcasted_iota(jnp.int32, (TILE, 128), 1)
    total = jnp.zeros((TILE, 128), F32)
    for h in range(HEADS):
        c = head(h)
        keys = jnp.concatenate([left[KEYS, c], k[:, c], right[KEYS, c]], axis=0)
        values = jnp.concatenate([left[VALUES, c], v[:, c], right[VALUES, c]], axis=0)
        s = dot(q[:, c], keys, NT) * SCALE + bias
        top = jnp.max(s, axis=1, keepdims=True)
        e = jnp.exp(s - top)
        mass = jnp.sum(e, axis=1, keepdims=True)
        p = (e * (1.0 / mass)).astype(BF16)
        att[:, c] = dot(p, values).astype(BF16)
        total = jnp.where(lane == h, top + jnp.log(mass), total)
        if (h + 1) * HEAD_DIM % SPAN == 0:
            n = (h + 1) * HEAD_DIM // SPAN - 1
            moved = dot(order[...], att[:, n * SPAN : (n + 1) * SPAN], NT).astype(BF16)
            rows = SPAN // GROUP
            for g in range(GROUP):
                att_t[g, n * rows : (n + 1) * rows, :] = moved[g * rows : (g + 1) * rows]
    stats[...] = total


def place(info, n):
    side, step = divmod(n, 4)
    core = info[4] if side == 0 else 1 - info[4]
    return core * 4 + lax.rem(info[5] + step, 4)


def spread_kernel(scalars, near, far, copies, outs, scratch):
    (info,), (out, w) = scalars, outs
    att_t, held, passed, *grads = near
    out[:, :GROUP_ROWS, :] = att_t[...]
    w[...] = jnp.where(info[4] == info[7], held[...], passed[...])
    for side in range(2):
        for n in range(0, 4, 2):
            pair = grads[side][n * TILE : (n + 2) * TILE, :]
            got = dot(w[...], pair, NT).astype(BF16)
            out[place(info, side * 4 + n), GROUP_ROWS:, :] = got[:, :TILE]
            out[place(info, side * 4 + n + 1), GROUP_ROWS:, :] = got[:, TILE:]


def weight_kernel(scalars, near, far, copies, outs, scratch):
    (info,), (mixed, *grads), (out,) = scalars, near, outs
    acc = None
    for side in range(2):
        rows = [mixed[place(info, side * 4 + n), :GROUP_ROWS, :] for n in range(4)]
        term = dot(jnp.concatenate(rows, axis=1), grads[side][...])
        acc = term if acc is None else acc + term
    out[...] = (acc * float(GROUP * TILES * TILE) ** -0.5).astype(BF16)


def delta_kernel(scalars, near, far, copies, outs, scratch):
    mixed, att, stats = near
    ga, out = outs
    lane = lax.broadcasted_iota(jnp.int32, (TILE, 128), 1)
    total = stats[...]
    rows = mixed[:, GROUP_ROWS:, :].reshape(HD, TILE)
    for h in range(HEADS):
        c = head(h)
        own = rows[c, :].T
        ga[:TILE, c] = own
        terms = own.astype(F32) * att[:, c].astype(F32)
        total = jnp.where(lane == HEADS + h, jnp.sum(terms, axis=1, keepdims=True), total)
    out[...] = total
    turned = total.T
    rest = [
        jnp.concatenate([turned[k * HEADS + h : k * HEADS + h + 1, :] for h in range(HEADS)], axis=1)
        for k in range(2)
    ]
    terms = []
    for _ in range(3):
        for k in range(2):
            part = rest[k].astype(BF16).astype(F32)
            rest[k] = rest[k] - part
            terms.append(part)
    terms.append(jnp.zeros((EXTRA - len(terms), HD), F32))
    ga[TILE:, :] = jnp.concatenate(terms, axis=0).astype(BF16)


def sum_kernel(scalars, near, far, copies, outs, scratch):
    (info,), (parts,) = scalars, near
    total = parts[0].astype(F32)
    for n in range(1, 8):
        total += parts[n].astype(F32)
    pieces = [total[n * ROWS_OUT : (n + 1) * ROWS_OUT, :] for n in range(4)]
    for step, ref in enumerate(outs):
        want = jnp.bitwise_xor(info[6], step)
        low = jnp.where(want == 0, pieces[0], pieces[1])
        high = jnp.where(want == 2, pieces[2], pieces[3])
        ref[...] = jnp.where(want < 2, low, high)


def project_kernel(scalars, near, far, copies, outs, scratch):
    (info,), (att, *blocks), (out,), (turned,) = scalars, near, outs, scratch
    for h in range(HEADS):
        turned[head(h), :] = att[:, head(h)].T
    acc = jnp.zeros((TILE, HD), F32)
    for n in range(GROUP):
        first = pl.multiple_of(place(info, n) * GROUP_ROWS, GROUP_ROWS)
        acc += dot(turned[pl.ds(first, GROUP_ROWS), :], blocks[n][...], TN)
    out[...] = acc.astype(BF16)


def backward_kernel(scalars, near, far, copies, outs, scratch):
    (info,), (stats,) = scalars, near
    q, k, v, left, right, ga, ql, qr, gal, gar = far
    (dq, dk, dv), sems, leaving = scratch[:3], scratch[3], []
    st = stats[...]
    for h in range(HEADS):
        if h % (HEADS // CHUNKS) == 0:
            for copy in copies[h // (HEADS // CHUNKS)]:
                copy.wait()
        if h == 0:
            on_row, on_column = row_bias(info, left, right), column_bias(info, left, right)
        c = head(h)
        keys = jnp.concatenate([left[KEYS, c], k[:, c], right[KEYS, c]], axis=0)
        values = jnp.concatenate([left[VALUES, c], v[:, c], right[VALUES, c]], axis=0)
        qh, gh = q[:, c], ga[:TILE, c]
        s = dot(qh, keys, NT) * SCALE + on_row
        p = jnp.exp(s - st[:, h : h + 1])
        dp = dot(gh, values, NT)
        ds = (p * (dp - st[:, HEADS + h : HEADS + h + 1]) * SCALE).astype(BF16)
        dq[:, c] = dot(ds, keys).astype(BF16)
        dkh = dot(ds[:, TILE : 2 * TILE], qh, TN)
        dvh = dot(p[:, TILE : 2 * TILE].astype(BF16), gh, TN)

        queries = jnp.concatenate([ql[:, c], qr[:, c]], axis=0)
        grads = jnp.concatenate([gal[:TILE, c], gar[:TILE, c]], axis=0)
        sent = [g[TILE:, c].astype(F32) for g in (gal, gar)]
        lse, delta = (
            jnp.concatenate([t[n : n + 1] + t[n + 2 : n + 3] + t[n + 4 : n + 5] for t in sent], axis=1)
            for n in range(2)
        )
        s = dot(k[:, c], queries, NT) * SCALE + on_column
        p = jnp.exp(s - lse)
        dp = dot(v[:, c], grads, NT)
        ds = (p * (dp - delta) * SCALE).astype(BF16)
        dk[:, c] = (dkh + dot(ds, queries)).astype(BF16)
        dv[:, c] = (dvh + dot(p.astype(BF16), grads)).astype(BF16)
        if (h + 1) % (HEADS // CHUNKS) == 0:
            chunk = h // (HEADS // CHUNKS)
            cols = pl.ds(chunk * (HD // CHUNKS), HD // CHUNKS)
            for n, (done, out) in enumerate(zip((dq, dk, dv), outs)):
                leaving.append(
                    pltpu.make_async_copy(done.at[:, cols], out.at[:, cols], sems.at[n, chunk])
                )
                leaving[-1].start()
    for copy in leaving:
        copy.wait()


def call(kernel, micros, scalars, near, far, outs, scratch=(), mib=4, chunks=1, place_out=VMEM):
    counts = [len(scalars), len(near), len(far), len(outs), len(far), len(scratch)]
    ends = np.cumsum(counts)

    def body(*refs):
        parts = [refs[end - count : end] for end, count in zip(ends, counts)]
        sems = refs[ends[-1]]
        copies = [[] for _ in range(chunks)]
        for chunk in range(chunks):
            for n, (ref, buffer) in enumerate(zip(parts[2], parts[4])):
                width = buffer.shape[-1] // chunks
                cols = (slice(None),) * (len(buffer.shape) - 1) + (pl.ds(chunk * width, width),)
                copy = pltpu.make_async_copy(ref.at[cols], buffer.at[cols], sems.at[n, chunk])
                copy.start()
                copies[chunk].append(copy)
        kernel(parts[0], parts[1], parts[4], copies if chunks > 1 else copies[0], parts[3], parts[5])

    return pl.pallas_call(
        body,
        in_specs=[pl.BlockSpec(memory_space=pltpu.SMEM)] * len(scalars)
        + [pl.BlockSpec(memory_space=VMEM)] * len(near)
        + [pl.BlockSpec(memory_space=pltpu.HBM)] * len(far),
        out_specs=[pl.BlockSpec(memory_space=place_out)] * len(outs),
        out_shape=[jax.ShapeDtypeStruct(s, d) for s, d in outs],
        scratch_shapes=[VMEM(f.shape, f.dtype) for f in far]
        + list(scratch)
        + [pltpu.SemaphoreType.DMA((max(1, len(far)), chunks))],
        cost_estimate=pl.CostEstimate(flops=int(micros * 1e9), bytes_accessed=1024, transcendentals=0),
        compiler_params=pltpu.CompilerParams(vmem_limit_bytes=mib * 1024 * 1024),
    )(*scalars, *near, *far)


def column_order():
    features = np.arange(SPAN).reshape(SPAN // 96, 2, 2, 4, ROWS_OUT)
    return np.eye(SPAN, dtype=np.float32)[features.transpose(1, 3, 0, 2, 4).reshape(-1)]


def shards(query_rows, key_rows, value_rows, frame_of, reach_back, reach_ahead, out_weight, out_grad):
    core = lax.axis_index("core")
    q, k, v, og = query_rows[0], key_rows[0], value_rows[0], out_grad[0]
    tile = (TILE, HD)
    where = (lax.axis_index(FRAME), core, lax.axis_index("x"), lax.axis_index(("yhi", "ylo")))
    where = where + (lax.axis_index("ylo"),)
    info = jnp.stack([frame_of[0, 0], reach_back[0, 0], reach_ahead[0, 0], *where]).astype(jnp.int32)

    to_send = pack(frame_of, reach_back, reach_ahead, k, v)
    left, right = next_tile(to_send, 1), next_tile(to_send, -1)

    w_passed = lax.ppermute(out_weight, ("core", "ylo"), [(0, 1), (3, 2)])

    og_sent = after(og, to_send)
    og_mine = join([og] + [along_x(og_sent, step) for step in (1, 2, 3)])
    og_other = core_swap(og_mine)

    order = jnp.asarray(column_order(), BF16)
    att, att_t, stats = call(
        forward_kernel,
        8,
        (info,),
        (q, k, v, left, right, order),
        (),
        [(tile, BF16), ((GROUP, GROUP_ROWS, TILE), BF16), ((TILE, 128), F32)],
        mib=8,
    )

    q2 = after(q, att)
    ql, qr = next_tile(q2, 1), next_tile(q2, -1)

    mixed, w_block = call(
        spread_kernel,
        2,
        (info,),
        (att_t, out_weight, w_passed, og_mine, og_other),
        (),
        [((GROUP, 2 * GROUP_ROWS, TILE), BF16), ((GROUP_ROWS, HD), BF16)],
    )
    blocks = [w_block, along_x(w_block, 1), None, along_x(w_block, 3)]
    mixed = lax.all_to_all(mixed, ("core", "x"), 0, 0, tiled=True)

    ga, stats = call(
        delta_kernel,
        1,
        (),
        (mixed, att, stats),
        (),
        [((TILE + EXTRA, HD), BF16), ((TILE, 128), F32)],
    )
    gal, gar = next_tile(ga, 1), next_tile(ga, -1)

    (partial,) = call(
        weight_kernel,
        2,
        (info,),
        (after(mixed, ga, ql, qr), og_mine, og_other),
        (),
        [((GROUP_ROWS, HD), BF16)],
    )
    along_z = lax.all_to_all(partial.reshape(8, GROUP_ROWS // 8, HD), "z", 0, 0, tiled=True)

    blocks[2] = along_x(after(w_block, partial), 2)

    dq, dk, dv = call(
        backward_kernel,
        9,
        (info,),
        (after(stats, partial, blocks[1], blocks[3]),),
        (q, k, v, left, right, ga, ql, qr, gal, gar),
        [(tile, BF16)] * 3,
        scratch=[VMEM(tile, BF16)] * 3 + [pltpu.SemaphoreType.DMA((3, CHUNKS))],
        mib=56,
        chunks=CHUNKS,
        place_out=pltpu.HBM,
    )
    blocks = blocks + [core_swap(after(w, dq)) for w in blocks]

    pieces = call(
        sum_kernel,
        1,
        (info,),
        (after(along_z, dq),),
        (),
        [((ROWS_OUT, HD), F32)] * 4,
    )
    arrived = []
    for step in (1, 2, 3):
        pairs = [(i, i ^ step) for i in range(4)]
        arrived.append(lax.ppermute(pieces[step], ("yhi", "ylo"), pairs))

    (layer_out,) = call(
        project_kernel,
        4,
        (info,),
        (after(att, pieces[0]), *blocks),
        (),
        [(tile, BF16)],
        scratch=[VMEM((HD, TILE), BF16)],
    )
    grad_weight = after(pieces[0], layer_out) + arrived[0] + arrived[1] + arrived[2]
    return layer_out[None], dq[None], dk[None], dv[None], grad_weight


def solution(mesh):
    fine = jax.sharding.Mesh(np.asarray(mesh.devices).reshape(SIZES), NAMES)
    tokens = P(FSDP, FRAME, None)
    tiles = P(FSDP, FRAME)
    in_specs = (tokens, tokens, tokens, tiles, tiles, tiles, P(FSDP, None), tokens)
    out_specs = (tokens, tokens, tokens, tokens, P(FRAME + FSDP, None))
    return jax.shard_map(shards, mesh=fine, in_specs=in_specs, out_specs=out_specs, check_vma=False)
```

```python
import jax
import jax.numpy as jnp
import numpy as np
from jax import lax
from jax.experimental import pallas as pl
from jax.experimental.pallas import tpu as pltpu
from jax.sharding import PartitionSpec as P

HEADS = 12
HEAD_DIM = 128
TILE = 128
HD = HEADS * HEAD_DIM
SCALE = HEAD_DIM**-0.5
MASKED = -1e30

SIZES = (8, 2, 2, 2, 4)
NAMES = ("z", "yhi", "core", "ylo", "x")
FRAME = ("z", "yhi", "core")
FSDP = ("ylo", "x")
TILES = 32
ROWS_OUT = 6
GROUP = 8
GROUP_ROWS = HD // GROUP
EXTRA = 16
SPAN = 384
CHUNKS = 4

F32 = jnp.float32
BF16 = jnp.bfloat16
VMEM = pltpu.VMEM
NT = (((1,), (1,)), ((), ()))
NN = (((1,), (0,)), ((), ()))
TN = (((0,), (0,)), ((), ()))


def dot(a, b, dims=NN):
    return lax.dot_general(a, b, dims, preferred_element_type=F32)


def next_tile(value, step):
    return lax.ppermute(value, FRAME, [(i, (i + step) % TILES) for i in range(TILES)])


def core_swap(value):
    return lax.ppermute(value, "core", [(0, 1), (1, 0)])


def along_x(value, step):
    return lax.ppermute(value, "x", [((i + step) % 4, i) for i in range(4)])


def along_x(value, step):
    return lax.ppermute(value, "x", [((i + step) % 4, i) for i in range(4)])


def after(value, *others):
    return lax.optimization_barrier((value, *others))[0]


def head(h):
    return slice(h * HEAD_DIM, (h + 1) * HEAD_DIM)


def visible(frame, low, high, there):
    seen = (frame >= low) & (frame <= high)
    return jnp.minimum(jnp.where(seen, 0.0, MASKED), jnp.where(there, 0.0, MASKED))


def told(tile):
    row = tile[2 * TILE : 2 * TILE + EXTRA, :HEAD_DIM].astype(F32)[:1]
    return row[:, 0:1], row[:, 1:2], row[:, 2:3]


def row_bias(info, left, right):
    frame, back, ahead = (info[n].astype(F32) for n in range(3))
    low, high, position = frame - back, frame + ahead, info[3]
    column = lax.broadcasted_iota(jnp.int32, (1, 3 * TILE), 1)
    on_left = visible(told(left)[0], low, high, position > 0)
    on_right = visible(told(right)[0], low, high, position < TILES - 1)
    return jnp.where(column < TILE, on_left, jnp.where(column < 2 * TILE, 0.0, on_right))


def column_bias(info, left, right):
    frame, position = info[0].astype(F32), info[3]
    column = lax.broadcasted_iota(jnp.int32, (1, 2 * TILE), 1)
    sides = []
    for tile, there in ((left, position > 0), (right, position < TILES - 1)):
        center, back, ahead = told(tile)
        sides.append(visible(frame, center - back, center + ahead, there))
    return jnp.where(column < TILE, sides[0], sides[1])


KEYS = slice(0, TILE)
VALUES = slice(TILE, 2 * TILE)


def pack_kernel(frame, back, ahead, k, v, out, sems):
    copies = [
        pltpu.make_async_copy(k, out.at[KEYS], sems.at[0]),
        pltpu.make_async_copy(v, out.at[VALUES], sems.at[1]),
    ]
    for copy in copies:
        copy.start()
    lane = lax.broadcasted_iota(jnp.int32, (EXTRA, HD), 1)
    said = jnp.where(lane == 0, frame[0, 0], jnp.where(lane == 1, back[0, 0], ahead[0, 0]))
    out[2 * TILE :, :] = said.astype(F32).astype(BF16)
    for copy in copies:
        copy.wait()


def pack(frame, back, ahead, k, v):
    return pl.pallas_call(
        pack_kernel,
        in_specs=[pl.BlockSpec(memory_space=pltpu.SMEM)] * 3 + [pl.BlockSpec(memory_space=pltpu.HBM)] * 2,
        out_specs=pl.BlockSpec(memory_space=VMEM),
        out_shape=jax.ShapeDtypeStruct((2 * TILE + EXTRA, HD), BF16),
        scratch_shapes=[pltpu.SemaphoreType.DMA((2,))],
        compiler_params=pltpu.CompilerParams(vmem_limit_bytes=56 * 1024 * 1024),
    )(frame, back, ahead, k, v)


def join_kernel(*refs):
    parts, out, sems = refs[:-2], refs[-2], refs[-1]
    copies = [
        pltpu.make_async_copy(part, out.at[n * TILE : (n + 1) * TILE], sems.at[n])
        for n, part in enumerate(parts)
    ]
    for copy in copies:
        copy.start()
    for copy in copies:
        copy.wait()


def join(parts):
    return pl.pallas_call(
        join_kernel,
        in_specs=[pl.BlockSpec(memory_space=pltpu.HBM)] * len(parts),
        out_specs=pl.BlockSpec(memory_space=VMEM),
        out_shape=jax.ShapeDtypeStruct((len(parts) * TILE, HD), BF16),
        scratch_shapes=[pltpu.SemaphoreType.DMA((len(parts),))],
        cost_estimate=pl.CostEstimate(flops=1024, bytes_accessed=1024, transcendentals=0),
        compiler_params=pltpu.CompilerParams(vmem_limit_bytes=4 * 1024 * 1024),
    )(*parts)


def forward_kernel(scalars, near, far, copies, outs, scratch):
    (info,) = scalars
    q, k, v, left, right, order = near
    att, att_t, stats = outs
    bias = row_bias(info, left, right)
    lane = lax.broadcasted_iota(jnp.int32, (TILE, 128), 1)
    total = jnp.zeros((TILE, 128), F32)
    for h in range(HEADS):
        c = head(h)
        keys = jnp.concatenate([left[KEYS, c], k[:, c], right[KEYS, c]], axis=0)
        values = jnp.concatenate([left[VALUES, c], v[:, c], right[VALUES, c]], axis=0)
        s = dot(q[:, c], keys, NT) * SCALE + bias
        top = jnp.max(s, axis=1, keepdims=True)
        e = jnp.exp(s - top)
        mass = jnp.sum(e, axis=1, keepdims=True)
        p = (e * (1.0 / mass)).astype(BF16)
        att[:, c] = dot(p, values).astype(BF16)
        total = jnp.where(lane == h, top + jnp.log(mass), total)
        if (h + 1) * HEAD_DIM % SPAN == 0:
            n = (h + 1) * HEAD_DIM // SPAN - 1
            moved = dot(order[...], att[:, n * SPAN : (n + 1) * SPAN], NT).astype(BF16)
            rows = SPAN // GROUP
            for g in range(GROUP):
                att_t[g, n * rows : (n + 1) * rows, :] = moved[g * rows : (g + 1) * rows]
    stats[...] = total


def place(info, n):
    side, step = divmod(n, 4)
    core = info[4] if side == 0 else 1 - info[4]
    return core * 4 + lax.rem(info[5] + step, 4)


def spread_kernel(scalars, near, far, copies, outs, scratch):
    (info,), (out, w) = scalars, outs
    att_t, held, passed, *grads = near
    out[:, :GROUP_ROWS, :] = att_t[...]
    w[...] = jnp.where(info[4] == info[7], held[...], passed[...])
    for side in range(2):
        for n in range(0, 4, 2):
            pair = grads[side][n * TILE : (n + 2) * TILE, :]
            got = dot(w[...], pair, NT).astype(BF16)
            out[place(info, side * 4 + n), GROUP_ROWS:, :] = got[:, :TILE]
            out[place(info, side * 4 + n + 1), GROUP_ROWS:, :] = got[:, TILE:]


def weight_kernel(scalars, near, far, copies, outs, scratch):
    (info,), (mixed, *grads), (out,) = scalars, near, outs
    acc = None
    for side in range(2):
        rows = [mixed[place(info, side * 4 + n), :GROUP_ROWS, :] for n in range(4)]
        term = dot(jnp.concatenate(rows, axis=1), grads[side][...])
        acc = term if acc is None else acc + term
    out[...] = (acc * float(GROUP * TILES * TILE) ** -0.5).astype(BF16)


def delta_kernel(scalars, near, far, copies, outs, scratch):
    mixed, att, stats = near
    ga, out = outs
    lane = lax.broadcasted_iota(jnp.int32, (TILE, 128), 1)
    total = stats[...]
    rows = mixed[:, GROUP_ROWS:, :].reshape(HD, TILE)
    for h in range(HEADS):
        c = head(h)
        own = rows[c, :].T
        ga[:TILE, c] = own
        terms = own.astype(F32) * att[:, c].astype(F32)
        total = jnp.where(lane == HEADS + h, jnp.sum(terms, axis=1, keepdims=True), total)
    out[...] = total
    turned = total.T
    rest = [
        jnp.concatenate([turned[k * HEADS + h : k * HEADS + h + 1, :] for h in range(HEADS)], axis=1)
        for k in range(2)
    ]
    terms = []
    for _ in range(3):
        for k in range(2):
            part = rest[k].astype(BF16).astype(F32)
            rest[k] = rest[k] - part
            terms.append(part)
    terms.append(jnp.zeros((EXTRA - len(terms), HD), F32))
    ga[TILE:, :] = jnp.concatenate(terms, axis=0).astype(BF16)


def sum_kernel(scalars, near, far, copies, outs, scratch):
    (info,), (parts,) = scalars, near
    total = parts[0].astype(F32)
    for n in range(1, 8):
        total += parts[n].astype(F32)
    pieces = [total[n * ROWS_OUT : (n + 1) * ROWS_OUT, :] for n in range(4)]
    for step, ref in enumerate(outs):
        want = jnp.bitwise_xor(info[6], step)
        low = jnp.where(want == 0, pieces[0], pieces[1])
        high = jnp.where(want == 2, pieces[2], pieces[3])
        ref[...] = jnp.where(want < 2, low, high)


def project_kernel(scalars, near, far, copies, outs, scratch):
    (info,), (att, *blocks), (out,), (turned,) = scalars, near, outs, scratch
    for h in range(HEADS):
        turned[head(h), :] = att[:, head(h)].T
    acc = jnp.zeros((TILE, HD), F32)
    for n in range(GROUP):
        first = pl.multiple_of(place(info, n) * GROUP_ROWS, GROUP_ROWS)
        acc += dot(turned[pl.ds(first, GROUP_ROWS), :], blocks[n][...], TN)
    out[...] = acc.astype(BF16)


def backward_kernel(scalars, near, far, copies, outs, scratch):
    (info,), (stats,) = scalars, near
    q, k, v, left, right, ga, ql, qr, gal, gar = far
    (dq, dk, dv), sems, leaving = scratch[:3], scratch[3], []
    st = stats[...]
    for h in range(HEADS):
        if h % (HEADS // CHUNKS) == 0:
            for copy in copies[h // (HEADS // CHUNKS)]:
                copy.wait()
        if h == 0:
            on_row, on_column = row_bias(info, left, right), column_bias(info, left, right)
        c = head(h)
        keys = jnp.concatenate([left[KEYS, c], k[:, c], right[KEYS, c]], axis=0)
        values = jnp.concatenate([left[VALUES, c], v[:, c], right[VALUES, c]], axis=0)
        qh, gh = q[:, c], ga[:TILE, c]
        s = dot(qh, keys, NT) * SCALE + on_row
        p = jnp.exp(s - st[:, h : h + 1])
        dp = dot(gh, values, NT)
        ds = (p * (dp - st[:, HEADS + h : HEADS + h + 1]) * SCALE).astype(BF16)
        dq[:, c] = dot(ds, keys).astype(BF16)
        dkh = dot(ds[:, TILE : 2 * TILE], qh, TN)
        dvh = dot(p[:, TILE : 2 * TILE].astype(BF16), gh, TN)

        queries = jnp.concatenate([ql[:, c], qr[:, c]], axis=0)
        grads = jnp.concatenate([gal[:TILE, c], gar[:TILE, c]], axis=0)
        sent = [g[TILE:, c].astype(F32) for g in (gal, gar)]
        lse, delta = (
            jnp.concatenate([t[n : n + 1] + t[n + 2 : n + 3] + t[n + 4 : n + 5] for t in sent], axis=1)
            for n in range(2)
        )
        s = dot(k[:, c], queries, NT) * SCALE + on_column
        p = jnp.exp(s - lse)
        dp = dot(v[:, c], grads, NT)
        ds = (p * (dp - delta) * SCALE).astype(BF16)
        dk[:, c] = (dkh + dot(ds, queries)).astype(BF16)
        dv[:, c] = (dvh + dot(p.astype(BF16), grads)).astype(BF16)
        if (h + 1) % (HEADS // CHUNKS) == 0:
            chunk = h // (HEADS // CHUNKS)
            cols = pl.ds(chunk * (HD // CHUNKS), HD // CHUNKS)
            for n, (done, out) in enumerate(zip((dq, dk, dv), outs)):
                leaving.append(
                    pltpu.make_async_copy(done.at[:, cols], out.at[:, cols], sems.at[n, chunk])
                )
                leaving[-1].start()
    for copy in leaving:
        copy.wait()


def call(kernel, micros, scalars, near, far, outs, scratch=(), mib=4, chunks=1, place_out=VMEM):
    counts = [len(scalars), len(near), len(far), len(outs), len(far), len(scratch)]
    ends = np.cumsum(counts)

    def body(*refs):
        parts = [refs[end - count : end] for end, count in zip(ends, counts)]
        sems = refs[ends[-1]]
        copies = [[] for _ in range(chunks)]
        for chunk in range(chunks):
            for n, (ref, buffer) in enumerate(zip(parts[2], parts[4])):
                width = buffer.shape[-1] // chunks
                cols = (slice(None),) * (len(buffer.shape) - 1) + (pl.ds(chunk * width, width),)
                copy = pltpu.make_async_copy(ref.at[cols], buffer.at[cols], sems.at[n, chunk])
                copy.start()
                copies[chunk].append(copy)
        kernel(parts[0], parts[1], parts[4], copies if chunks > 1 else copies[0], parts[3], parts[5])

    return pl.pallas_call(
        body,
        in_specs=[pl.BlockSpec(memory_space=pltpu.SMEM)] * len(scalars)
        + [pl.BlockSpec(memory_space=VMEM)] * len(near)
        + [pl.BlockSpec(memory_space=pltpu.HBM)] * len(far),
        out_specs=[pl.BlockSpec(memory_space=place_out)] * len(outs),
        out_shape=[jax.ShapeDtypeStruct(s, d) for s, d in outs],
        scratch_shapes=[VMEM(f.shape, f.dtype) for f in far]
        + list(scratch)
        + [pltpu.SemaphoreType.DMA((max(1, len(far)), chunks))],
        cost_estimate=pl.CostEstimate(flops=int(micros * 25e8), bytes_accessed=1024, transcendentals=0),
        compiler_params=pltpu.CompilerParams(vmem_limit_bytes=mib * 1024 * 1024),
    )(*scalars, *near, *far)


def column_order():
    features = np.arange(SPAN).reshape(SPAN // 96, 2, 2, 4, ROWS_OUT)
    return np.eye(SPAN, dtype=np.float32)[features.transpose(1, 3, 0, 2, 4).reshape(-1)]


def shards(query_rows, key_rows, value_rows, frame_of, reach_back, reach_ahead, out_weight, out_grad):
    core = lax.axis_index("core")
    q, k, v, og = query_rows[0], key_rows[0], value_rows[0], out_grad[0]
    tile = (TILE, HD)
    where = (lax.axis_index(FRAME), core, lax.axis_index("x"), lax.axis_index(("yhi", "ylo")))
    where = where + (lax.axis_index("ylo"),)
    info = jnp.stack([frame_of[0, 0], reach_back[0, 0], reach_ahead[0, 0], *where]).astype(jnp.int32)

    to_send = pack(frame_of, reach_back, reach_ahead, k, v)
    left, right = next_tile(to_send, 1), next_tile(to_send, -1)

    w_passed = lax.ppermute(out_weight, ("core", "ylo"), [(0, 1), (3, 2)])

    og_sent = after(og, to_send)
    og_mine = join([og] + [along_x(og_sent, step) for step in (1, 2, 3)])
    og_other = core_swap(og_mine)

    order = jnp.asarray(column_order(), BF16)
    att, att_t, stats = call(
        forward_kernel,
        8,
        (info,),
        (q, k, v, left, right, order),
        (),
        [(tile, BF16), ((GROUP, GROUP_ROWS, TILE), BF16), ((TILE, 128), F32)],
        mib=8,
    )

    q2 = after(q, att)
    ql, qr = next_tile(q2, 1), next_tile(q2, -1)

    mixed, w_block = call(
        spread_kernel,
        2,
        (info,),
        (att_t, out_weight, w_passed, og_mine, og_other),
        (),
        [((GROUP, 2 * GROUP_ROWS, TILE), BF16), ((GROUP_ROWS, HD), BF16)],
    )
    blocks = [w_block, along_x(w_block, 1), None, along_x(w_block, 3)]
    mixed = lax.all_to_all(mixed, ("core", "x"), 0, 0, tiled=True)

    ga, stats = call(
        delta_kernel,
        1,
        (),
        (mixed, att, stats),
        (),
        [((TILE + EXTRA, HD), BF16), ((TILE, 128), F32)],
    )
    gal, gar = next_tile(ga, 1), next_tile(ga, -1)

    (partial,) = call(
        weight_kernel,
        2,
        (info,),
        (after(mixed, ga, ql, qr), og_mine, og_other),
        (),
        [((GROUP_ROWS, HD), BF16)],
    )
    along_z = lax.all_to_all(partial.reshape(8, GROUP_ROWS // 8, HD), "z", 0, 0, tiled=True)

    blocks[2] = along_x(after(w_block, partial), 2)

    dq, dk, dv = call(
        backward_kernel,
        9,
        (info,),
        (after(stats, partial, blocks[1], blocks[3]),),
        (q, k, v, left, right, ga, ql, qr, gal, gar),
        [(tile, BF16)] * 3,
        scratch=[VMEM(tile, BF16)] * 3 + [pltpu.SemaphoreType.DMA((3, CHUNKS))],
        mib=56,
        chunks=CHUNKS,
        place_out=pltpu.HBM,
    )
    blocks = blocks + [core_swap(after(w, dq)) for w in blocks]

    pieces = call(
        sum_kernel,
        1,
        (info,),
        (after(along_z, dq),),
        (),
        [((ROWS_OUT, HD), F32)] * 4,
    )
    arrived = []
    for step in (1, 2, 3):
        pairs = [(i, i ^ step) for i in range(4)]
        arrived.append(lax.ppermute(pieces[step], ("yhi", "ylo"), pairs))

    (layer_out,) = call(
        project_kernel,
        4,
        (info,),
        (after(att, pieces[0]), *blocks),
        (),
        [(tile, BF16)],
        scratch=[VMEM((HD, TILE), BF16)],
    )
    grad_weight = after(pieces[0], layer_out) + arrived[0] + arrived[1] + arrived[2]
    return layer_out[None], dq[None], dk[None], dv[None], grad_weight


def solution(mesh):
    fine = jax.sharding.Mesh(np.asarray(mesh.devices).reshape(SIZES), NAMES)
    tokens = P(FSDP, FRAME, None)
    tiles = P(FSDP, FRAME)
    in_specs = (tokens, tokens, tokens, tiles, tiles, tiles, P(FSDP, None), tokens)
    out_specs = (tokens, tokens, tokens, tokens, P(FRAME + FSDP, None))
    return jax.shard_map(shards, mesh=fine, in_specs=in_specs, out_specs=out_specs, check_vma=False)
```
